512 devices in a mesh: blk: 8 (over y_hi, core), group: 64 (over z, y_lo, x).
Axes of the slice: x: 4, y: 8 (y_hi: 4, y_lo: 2; y = y_hi * 2 + y_lo), z: 8, core: 2. Of those that a mesh axis runs over, the one named last changes fastest.
Arguments:
- query_states: bfloat16 [36864, 4096], P(('blk', 'group')), may hold values from -6 to 6
- passage_states: bfloat16 [36864, 4096], P(('blk', 'group')), may hold values from -6 to 6
- norm_gain: float32 [4096], replicated, may hold values from 0.5 to 1.5
- negative_owner: int32 [36864, 4], P(('blk', 'group')), may hold values from 0 to 63, all different within a row; in each aligned block of 72 rows (0 to 71, 72 to 143, ...) at most 5 rows name the same one
- negative_row: int32 [36864, 4], P(('blk', 'group')), may hold values from 0 to 71
Outputs:
- query_grad: float32 [36864, 4096], P(('blk', 'group'))
- passage_grad: float32 [36864, 4096], P(('blk', 'group'))
- gain_grad: float32 [4096], replicated
- loss: float32 [], replicated
The draws below stay inside these ranges and needn't reach their ends.
Inputs may be any that keep to these rules, and one draw needn't show every extreme that they name: `negative_owner`: the 4 owners of one query are distinct. Among the rows of one device, no owner is named by more than 5 rows.
All inputs are finite; a program needn't handle non-finite values.
Results may differ from the reference program's by a relative error of at most 0.0018.
The reference program's roundings to bfloat16 on the way count: a program that leaves them out, or rounds other values in their place, can miss the bound.
Values may be sent and summed in bfloat16 or wider, within the bound.
A program may use at most 64 MiB of HBM per device.

```python
import math
import jax
import jax.numpy as jnp
import numpy as np
from jax import lax

D = 4096
BATCH_DEV = 72
NEGATIVES = 4
OWNERS = 64
CAPACITY = 5
BATCH = 36864
N_BLK = 8
N_GROUP = 64


def state_bases(key):
    normal_key = jax.random.fold_in(key, 1)
    normal_base = jnp.clip(jax.random.normal(normal_key, (BATCH, D), jnp.float32), -6.0, 6.0)
    return normal_base


def draw_passage_states(key, part):
    normal_base = state_bases(key)
    values = normal_base
    return values.astype(jnp.bfloat16)


def draw_query_states(key, part):
    key = jax.random.fold_in(key, 12)
    values = jnp.clip(jax.random.normal(key, (BATCH, D), jnp.float32), -6.0, 6.0)
    return values.astype(jnp.bfloat16)


def touch_ends(result, own_key, smallest, high):
    longest = result.shape.index(max(result.shape))
    spots = []
    for shift in (0, 1):
        where = [jax.random.randint(jax.random.fold_in(own_key, axis), (), 0, length) for axis, length in enumerate(result.shape)]
        where[longest] = (where[longest] + shift) % result.shape[longest]
        spots.append(tuple(where))
    return result.at[spots[0]].set(smallest).at[spots[1]].set(high)


def deal_out(own_key, own, number, rows, number_of, top, most, skew):
    order = jax.random.permutation(own_key, number_of)
    packed, usual = shares(number_of, rows * top, most, skew, True), shares(number_of, rows * top, most, skew, False)
    places = jnp.arange(number_of)

    def named(lengths, turn):
        used = int((lengths > 0).sum())
        fixed = max(1, used // 4)
        passed = fixed + (places - fixed + turn * (used - fixed)) % max(1, number_of - fixed)
        return jnp.zeros((number_of,), jnp.int32).at[order[jnp.where(places < fixed, places, passed)]].set(jnp.asarray(lengths, jnp.int32))

    lengths = jnp.where(number % 4 == 0, named(packed, number // 4), named(usual, number - number // 4 - 1))
    mixed = jax.random.permutation(jax.random.fold_in(own, 3), number_of)
    donor, taker = mixed[0:number_of // 2 * 2:2], mixed[1:number_of // 2 * 2:2]
    margin = jnp.minimum(lengths[donor] - 1, most - lengths[taker]) // 2
    margin = jnp.where((donor == order[0]) | (taker == order[0]) | (lengths[taker] == 0), 0, jnp.maximum(margin, 0))
    passed = jax.random.randint(jax.random.fold_in(own, 4), (number_of // 2,), 0, 1 << 20) % (margin + 1)
    lengths = lengths.at[donor].add(-passed).at[taker].add(passed)
    members = jnp.searchsorted(jnp.cumsum(lengths), jnp.arange(rows * top), side="right").astype(jnp.int32)
    listing = members.reshape(top, rows).T
    listing = listing[jax.random.permutation(jax.random.fold_in(own, 1), rows)]
    turn = jax.random.randint(jax.random.fold_in(own, 2), (rows, 1), 0, top)
    return jnp.take_along_axis(listing, (jnp.arange(top)[None, :] + turn) % top, axis=1)


def shares(number_of, total, most, skew, full):
    portions = [(1 << 20) // math.isqrt(grade ** skew) + 1 for grade in range(1, number_of + 1)]
    largest = most if full else min(most, max(-(-total // number_of), total * portions[0] // sum(portions)))
    least = 1 if total - largest >= number_of - 1 else 0
    holding, surplus = [largest] + [least] * (number_of - 1), total - largest - least * (number_of - 1)
    while surplus > 0:
        candidates = [i for i in range(1, number_of) if holding[i] < largest] or [i for i in range(1, number_of) if holding[i] < most]
        mass, budget = sum([portions[i] for i in candidates]), surplus
        for i in candidates:
            more = min(most - holding[i], max(1, budget * portions[i] // mass), surplus)
            holding[i] = holding[i] + more
            surplus = surplus - more
    return np.array(holding)


def setup_inputs(seed: int = 0) -> dict:
    splits = jax.random.split(jax.random.key(seed), 6)
    query_states = draw_query_states(jax.random.fold_in(splits[5], 71), 0)
    passage_states = draw_passage_states(jax.random.fold_in(splits[5], 71), 0)
    norm_gain = jnp.clip(1.0 + 0.1 * jax.random.normal(splits[2], (D,), jnp.float32), 0.5, 1.5)
    negative_owner_keys = jax.random.split(jax.random.fold_in(splits[3], 1), BATCH // BATCH_DEV)
    negative_owner_turns = jax.random.permutation(jax.random.fold_in(splits[3], 3), BATCH // BATCH_DEV)
    negative_owner = jax.vmap(lambda own, number: deal_out(jax.random.fold_in(splits[3], 2), own, number, BATCH_DEV, OWNERS, NEGATIVES, CAPACITY, 2))(negative_owner_keys, negative_owner_turns).reshape((BATCH, NEGATIVES))
    negative_row = touch_ends(jax.random.randint(splits[4], (BATCH, NEGATIVES), 0, BATCH_DEV), jax.random.fold_in(splits[4], 1), 0, BATCH_DEV - 1).astype(jnp.int32)
    return {"query_states": query_states, "passage_states": passage_states, "norm_gain": norm_gain, "negative_owner": negative_owner, "negative_row": negative_row}


EPSILON = 1e-05

def embed_rows(states, gain_vector):
    values = states.astype(jnp.float32)
    inverse = lax.rsqrt(lax.optimization_barrier(jnp.mean(values * values, axis=-1, keepdims=True)) + EPSILON)
    return ((values * inverse * gain_vector).astype(jnp.bfloat16), inverse)

def norm_backward(states, inverse, gain_vector, upstream):
    values = states.astype(jnp.float32)
    scaled = gain_vector * upstream
    inner_sum = lax.optimization_barrier(jnp.sum(scaled * values, axis=-1, keepdims=True))
    grad_states = scaled * inverse - values * inverse ** 3 * inner_sum / values.shape[-1]
    grad_gain = lax.optimization_barrier(jnp.sum(upstream * values * inverse, axis=0))
    return (grad_states, grad_gain)

def reference(query_states, passage_states, norm_gain, negative_owner, negative_row):
    score_scale = 4.0 / math.sqrt(D)
    devices = N_BLK * N_GROUP
    query_embed, query_inverse = embed_rows(query_states, norm_gain)
    passage_embed, passage_inverse = embed_rows(passage_states, norm_gain)
    query_blocks = query_embed.reshape(N_BLK, N_GROUP, BATCH_DEV, D)
    passage_blocks = passage_embed.reshape(N_BLK, N_GROUP, BATCH_DEV, D)
    owner_lists = negative_owner.reshape(N_BLK, N_GROUP, BATCH_DEV * NEGATIVES)
    row_lists = negative_row.reshape(N_BLK, N_GROUP, BATCH_DEV * NEGATIVES)
    local_ids = jnp.arange(BATCH_DEV, dtype=jnp.int32)
    columns = jnp.arange(N_BLK * BATCH_DEV, dtype=jnp.int32)

    def forward(pool_total, device):
        blk_index = device // N_GROUP
        group_index = device % N_GROUP
        queries = query_blocks[blk_index, group_index]
        in_batch = passage_blocks[:, group_index].reshape(N_BLK * BATCH_DEV, D)
        pool_ids = ((blk_index * N_GROUP + owner_lists[blk_index, group_index]) * BATCH_DEV + row_lists[blk_index, group_index]).astype(jnp.int32)
        pool_rows = passage_embed[pool_ids]
        batch_scores = jnp.dot(queries, in_batch.T, preferred_element_type=jnp.float32) * score_scale
        pool_scores = jnp.dot(queries, pool_rows.T, preferred_element_type=jnp.float32) * score_scale
        row_peak = jnp.maximum(lax.optimization_barrier(jnp.max(batch_scores, axis=1)), lax.optimization_barrier(jnp.max(pool_scores, axis=1)))[:, None]
        summed = (lax.optimization_barrier(jnp.sum(jnp.exp(batch_scores - row_peak), axis=1)) + lax.optimization_barrier(jnp.sum(jnp.exp(pool_scores - row_peak), axis=1)))[:, None]
        totals = row_peak + jnp.log(summed)
        positive_col = blk_index * BATCH_DEV + local_ids
        target = (columns[None, :] == positive_col[:, None]).astype(jnp.float32)
        positive_score = lax.optimization_barrier(jnp.sum(batch_scores * target, axis=1))
        batch_coefficient = (jnp.exp(batch_scores - totals) - target).astype(jnp.bfloat16)
        pool_coefficient = jnp.exp(pool_scores - totals).astype(jnp.bfloat16)
        grad_embed = score_scale * (jnp.dot(batch_coefficient, in_batch, preferred_element_type=jnp.float32) + jnp.dot(pool_coefficient, pool_rows, preferred_element_type=jnp.float32))
        pool_terms = (score_scale * jnp.dot(pool_coefficient.T, queries, preferred_element_type=jnp.float32)).astype(jnp.bfloat16)
        pool_total = pool_total.at[pool_ids].add(pool_terms.astype(jnp.float32))
        loss_part = jnp.sum(totals[:, 0] - positive_score)
        return (pool_total, (grad_embed, totals[:, 0], loss_part))
    pool_total, (query_embed_grad, row_total, loss_parts) = lax.scan(forward, jnp.zeros((BATCH, D), jnp.float32), jnp.arange(devices, dtype=jnp.int32))
    total_blocks = row_total.reshape(N_BLK, N_GROUP, BATCH_DEV)

    def backward(device):
        blk_index = device // N_GROUP
        group_index = device % N_GROUP
        passages = passage_blocks[blk_index, group_index]
        queries = query_blocks[:, group_index].reshape(N_BLK * BATCH_DEV, D)
        totals = total_blocks[:, group_index].reshape(N_BLK * BATCH_DEV, 1)
        scores = jnp.dot(queries, passages.T, preferred_element_type=jnp.float32) * score_scale
        positive_col = blk_index * BATCH_DEV + local_ids
        target = (columns[:, None] == positive_col[None, :]).astype(jnp.float32)
        coefficient = (jnp.exp(scores - totals) - target).astype(jnp.bfloat16)
        return score_scale * jnp.dot(coefficient.T, queries, preferred_element_type=jnp.float32)
    batch_grads = lax.map(backward, jnp.arange(devices, dtype=jnp.int32))
    passage_embed_grad = batch_grads.reshape(BATCH, D) + pool_total
    query_grad, gain_query = norm_backward(query_states, query_inverse, norm_gain, query_embed_grad.reshape(BATCH, D))
    passage_grad, gain_passage = norm_backward(passage_states, passage_inverse, norm_gain, passage_embed_grad)
    loss = jnp.sum(loss_parts) / BATCH
    return (query_grad, passage_grad, gain_query + gain_passage, loss)
```

```python
import math

import jax
import jax.numpy as jnp
from jax import lax
from jax.experimental import pallas as pl
from jax.experimental.pallas import tpu as pltpu
from jax.sharding import PartitionSpec as P

EPSILON = 1e-05
MESH = pl.DeviceIdType.MESH
NZ, NY, NX = 8, 2, 4
NGROUP = NZ * NY * NX
NPOS, NCORE = 4, 2
NBLK = NPOS * NCORE
ROWS, WIDTH = 72, 4096
PAD = 80
SLOTS = 5
POOL = NGROUP * SLOTS
CHUNKS = NZ // 2
CROWS = POOL // CHUNKS
PLANE = NY * NX
LANES = CHUNKS * 128
FOLD, FOLDW = 16, 256
HEAD, TAILW = 64, 2048
HEADS, TAILS = NBLK * HEAD, NBLK * FOLD
STRIP = 512
SCALE = 4.0 / math.sqrt(WIDTH)
GAINS = WIDTH + 128
VMEM_LIMIT = 60 * 1024 * 1024
BF, F32, I32 = jnp.bfloat16, jnp.float32, jnp.int32


def turn_z(place):
    odd, half = place % 2, place // 2
    return (1 - odd) * half + odd * (NZ - 1 - half)


def peer(me, turn, back=False):
    z, y, x = me // (NY * NX), (me // NX) % NY, me % NX
    dz, dy, dx = turn_z(turn // (NY * NX)), (turn // NX) % NY, turn % NX
    if back:
        dz, dx = NZ - dz, NX - dx
    return (((z + dz) % NZ) * NY + (y + dy) % NY) * NX + (x + dx) % NX


def turn_of(me, other):
    dz = (other // (NY * NX) - me // (NY * NX)) % NZ
    dy = ((other // NX) % NY - (me // NX) % NY) % NY
    dx = (other % NX - me % NX) % NX
    place = jnp.where(dz < NZ // 2, 2 * dz, 2 * (NZ - 1 - dz) + 1)
    return (place * NY + dy) * NX + dx


def remote(src, dst, send, recv, **where):
    return pltpu.make_async_remote_copy(
        src_ref=src, dst_ref=dst, send_sem=send, recv_sem=recv, device_id=where, device_id_type=MESH
    )


class Spread:
    def __init__(self, blk, head, tail, send, recv):
        pos, core = blk // NCORE, blk % NCORE
        self.own = blk
        self.right = ((pos + 1) % NPOS) * NCORE + core
        self.left = ((pos + 3) % NPOS) * NCORE + core
        self.far = ((pos + 2) % NPOS) * NCORE + core
        self.twin = pos * NCORE + 1 - core
        self.head, self.tail, self.send, self.recv = head, tail, send, recv
        self.started = []

    def copy(self, kind, slot, piece, target):
        if piece < 4 and kind in (0, 1, 3, 5):
            ref = self.head.at[slot, pl.ds(piece * FOLD, FOLD)]
        elif piece < 4:
            ref = self.head.at[slot]
        elif kind in (3, 5):
            ref = self.tail.at[slot, :, pl.ds((kind // 5) * (TAILW // 2), TAILW // 2)]
        else:
            ref = self.tail.at[slot]
        sems = self.send.at[kind, piece], self.recv.at[kind, piece]
        return remote(ref, ref, *sems, blk=target)

    def start(self, kind, slot, piece, target):
        copy = self.copy(kind, slot, piece, target)
        copy.start()
        self.started.append(copy)

    def arrived(self, kind, slot, piece):
        self.copy(kind, slot, piece, self.own).wait_recv()

    def hop(self, *pieces):
        for piece in pieces:
            self.start(0, self.own, piece, self.right)
            self.start(1, self.own, (2, 3, 0, 1, 4)[piece], self.left)

    def over(self, kind, slot):
        self.start(kind, slot, 0, self.twin)
        self.start(kind, slot, 4, self.twin)

    def relay(self, *pieces):
        for piece in pieces:
            self.arrived(0, self.left, piece)
            self.start(3, self.left, piece, self.right)
            other = (2, 3, 0, 1, 4)[piece]
            self.arrived(1, self.right, other)
            self.start(5, self.right, other, self.left)

    def pass_near(self):
        self.arrived(0, self.left, 2)
        self.arrived(0, self.left, 3)
        self.over(4, self.left)
        self.arrived(1, self.right, 0)
        self.arrived(1, self.right, 1)
        self.over(6, self.right)

    def pass_far(self):
        for piece in (0, 1, 4):
            self.arrived(3, self.far, piece)
        for piece in (2, 3, 4):
            self.arrived(5, self.far, piece)
        self.over(7, self.far)

    def finish(self):
        for kind in (2, 4, 6, 7):
            self.arrived(kind, self.twin, 0)
            self.arrived(kind, self.twin, 4)

    def sent(self):
        for copy in self.started:
            copy.wait_send()


class Swap:
    def __init__(self, me, src, dst, send, recv, back):
        self.me, self.src, self.dst, self.send, self.recv, self.back = me, src, dst, send, recv, back

    def each(self, chunk, first, count, act):
        @pl.loop(first, first + count)
        def _(plane):
            for side in range(2):
                turn = (2 * chunk + side) * PLANE + plane

                @pl.when(turn > 0)
                def _():
                    rows = pl.ds(turn * SLOTS, SLOTS)
                    act(
                        remote(
                            self.src.at[rows],
                            self.dst.at[rows],
                            self.send.at[turn],
                            self.recv.at[turn],
                            group=peer(self.me, turn, self.back),
                        )
                    )

    def start(self, chunk, half):
        self.each(chunk, half * (PLANE // 2), PLANE // 2, lambda copy: copy.start())

    def arrived(self, chunk):
        self.each(chunk, 0, PLANE, lambda copy: copy.wait_recv())

    def sent(self):
        @pl.loop(0, CHUNKS)
        def _(chunk):
            self.each(chunk, 0, PLANE, lambda copy: copy.wait_send())


def iota(shape, dim):
    return lax.broadcasted_iota(I32, shape, dim)


def rows_of(start, count=FOLD):
    return pl.ds(pl.multiple_of(start, FOLD), count)


def to_column(row, count):
    same = iota((count, 128), 0) == iota((count, 128), 1)
    return jnp.sum(jnp.where(same, jnp.broadcast_to(row, (count, 128)), 0), axis=1, keepdims=True)


def matmul(left, right):
    return jnp.dot(left, right, preferred_element_type=F32)


def matmul_t(left, right):
    return lax.dot_general(left, right, (((1,), (1,)), ((), ())), preferred_element_type=F32)


def embed(states, gain, out, inverses):
    @pl.loop(0, PAD // FOLD)
    def _(step):
        at = rows_of(step * FOLD)
        values = states[at, :].astype(F32)
        inverse = lax.rsqrt(jnp.mean(values * values, axis=-1, keepdims=True) + EPSILON)
        inverses[at, :] = inverse
        out[at, :] = (values * inverse * gain[...]).astype(BF)


def place_own(blk, embedded, head, tail):
    head[blk] = embedded[0:HEAD, :]
    last = embedded[HEAD:PAD, :]
    last = last.astype(F32)[0 : ROWS - HEAD]
    tail[blk] = jnp.concatenate([last[:, :TAILW], last[:, TAILW:]], axis=0).astype(BF)


def fold_rows(left, right, factor, swap, work, stage, flat, chunk):
    first = chunk * CROWS

    @pl.loop(0, FOLD)
    def _(k):
        cols = pl.ds(pl.multiple_of(k * FOLDW, FOLDW), FOLDW)
        found = matmul(left, right[:, cols])
        if factor is not None:
            found = factor * found
        found = found.astype(BF)
        if flat is not None:
            flat[rows_of(first, CROWS), cols] = found
        work[:, rows_of(k * FOLD), :] = found.reshape(CROWS // FOLD, FOLD, FOLDW)

    for g in range(CROWS // FOLD):
        folded = matmul(swap[...], work[g]).astype(BF)
        stage[pl.ds(first + g * FOLD, FOLD)] = folded.reshape(FOLD, FOLD, FOLDW)


def pair_scores(embedded, head, tail):
    main = matmul_t(embedded[...], head[...].reshape(HEADS, WIDTH)) * SCALE
    folded = tail[...].reshape(TAILS, TAILW)
    low = matmul_t(embedded[:, :TAILW], folded)
    high = matmul_t(embedded[:, TAILW:], folded)
    return main, (low + pltpu.roll(high, TAILS - (ROWS - HEAD), 1)) * SCALE


def pair_masks(blk):
    row, lane = iota((PAD, HEADS), 0), iota((PAD, HEADS), 1)
    main = (row < HEAD) & (lane == blk * HEAD + row)
    row, lane = iota((PAD, TAILS), 0), iota((PAD, TAILS), 1)
    valid = (lane // (ROWS - HEAD)) % 2 == 0
    rest = (row >= HEAD) & (row < ROWS) & (lane == blk * FOLD + row - HEAD)
    return main, rest, valid


def pair_grads(main, rest, head, tail, out, extra):
    low = rest.astype(BF)
    high = pltpu.roll(rest, ROWS - HEAD, 1).astype(BF)
    main = main.astype(BF)
    for part, coeff in enumerate((low, high)):

        @pl.loop(0, TAILW // STRIP)
        def _(step):
            near = pl.ds(pl.multiple_of(step * STRIP, STRIP), STRIP)
            cols = pl.ds(pl.multiple_of(part * TAILW + step * STRIP, STRIP), STRIP)
            found = matmul(main, head[:, :, cols].reshape(HEADS, STRIP))
            found = found + matmul(coeff, tail[:, :, near].reshape(TAILS, STRIP))
            if extra is not None:
                found = found + extra(cols)
            out[:, cols] = SCALE * found


def norm_backward(states, inverses, gain, upstream, out, gain_sum):
    @pl.loop(0, PAD // FOLD)
    def _(step):
        at = rows_of(step * FOLD)
        values, inverse, given = states[at, :].astype(F32), inverses[at, :], upstream[at, :]
        if out is not None:
            scaled = gain[...] * given
            inner = jnp.sum(scaled * values, axis=-1, keepdims=True)
            out[at, :] = scaled * inverse - values * inverse**3 * inner / WIDTH
        if gain_sum is not None:
            gain_sum[...] += given * values * inverse


def kernel(
    query, passage, gain, ask,
    query_grad, passage_grad, sums,
    query_embed, passage_embed, query_inv, passage_inv, swap,
    phead, ptail, qhead, qtail,
    asked, work, stage, landed, pool, pool_raw, pool_inv, pool_scores, pool_turned,
    terms, term_stage, term_landed,
    main_scores, rest_scores, total_out, totals, query_up, passage_up, gain_sum, held, run,
    ask_send, ask_recv, row_send, row_recv, term_send, term_recv,
    p_send, p_recv, q_send, q_recv, total_send, total_recv, sum_send, sum_recv,
):
    me, blk = lax.axis_index("group"), lax.axis_index("blk")
    z, plane = me // PLANE, me % PLANE
    barrier = pltpu.get_barrier_semaphore()

    @pl.loop(1, NGROUP)
    def _(turn):
        pl.semaphore_signal(barrier, inc=1, device_id={"group": peer(me, turn)}, device_id_type=MESH)

    for d in range(1, NBLK):
        pl.semaphore_signal(barrier, inc=1, device_id={"blk": (blk + d) % NBLK}, device_id_type=MESH)

    asked[0] = ask[...]
    embed(passage, gain, passage_embed, passage_inv)
    place_own(blk, passage_embed, phead, ptail)
    row, col = iota((FOLDW, FOLDW), 0), iota((FOLDW, FOLDW), 1)
    same = (row // FOLD == col % FOLD) & (row % FOLD == col // FOLD)
    swap[...] = jnp.where(same, 1.0, 0.0).astype(BF)
    pl.semaphore_wait(barrier, NGROUP - 1 + NBLK - 1)

    def asking(turn):
        return remote(
            ask, asked.at[turn], ask_send.at[turn], ask_recv.at[turn], group=peer(me, turn)
        )

    @pl.loop(1, NGROUP)
    def _(turn):
        asking(turn).start()

    ps = Spread(blk, phead, ptail, p_send, p_recv)
    qs = Spread(blk, qhead, qtail, q_send, q_recv)
    ps.hop(0, 1)
    embed(query, gain, query_embed, query_inv)
    place_own(blk, query_embed, qhead, qtail)

    @pl.loop(1, NGROUP)
    def _(turn):
        asking(turn).wait()

    lanes, turns = iota((NGROUP, 1, LANES), 2), iota((NGROUP, 1, LANES), 0)
    mine = (lanes // 128 == turns // 16) & ((lanes % 128) // SLOTS == turns % 16)
    wanted = jnp.sum(jnp.where(mine, asked[...], 0), axis=0)

    rows = Swap(me, stage, landed, row_send, row_recv, True)
    spread_steps = [
        lambda: ps.hop(4),
        lambda: ps.hop(2),
        lambda: ps.hop(3),
        lambda: ps.over(2, blk),
        lambda: ps.relay(0),
        lambda: ps.relay(1),
        lambda: ps.relay(4),
        lambda: ps.pass_near(),
    ]
    for step in range(CHUNKS):
        chunk = CHUNKS - 1 - step
        column = to_column(wanted[:, chunk * 128 : (chunk + 1) * 128], CROWS)
        pick = jnp.where(column - 1 == iota((CROWS, PAD), 1), 1.0, 0.0).astype(BF)
        fold_rows(pick, passage, None, swap, work, stage, None, chunk)
        for half in range(2):
            rows.start(chunk, half)
            spread_steps[2 * step + half]()
    landed[0:SLOTS] = stage[0:SLOTS]
    qs.hop(0, 1, 4)
    ps.pass_far()
    qs.hop(2, 3)
    qs.over(2, blk)
    ps.finish()

    main_hit, rest_hit, rest_valid = pair_masks(blk)
    main, rest = pair_scores(query_embed, phead, ptail)
    main_scores[...] = main
    rest_scores[...] = jnp.where(rest_valid, rest, -jnp.inf)

    for step in range(CHUNKS):
        chunk = CHUNKS - 1 - step
        rows.arrived(chunk)

        @pl.loop(0, CROWS // FOLD)
        def _(g):
            at = chunk * CROWS + g * FOLD
            tile = landed[pl.ds(at, FOLD)].reshape(FOLDW, FOLDW)
            flat = matmul(swap[...], tile)
            square = jnp.zeros((FOLD, FOLDW), F32)
            for k in range(FOLD):
                part = flat[k * FOLD : (k + 1) * FOLD]
                square = square + part * part
            inverse = lax.rsqrt(jnp.sum(square, axis=1, keepdims=True) / WIDTH + EPSILON)
            pool_inv[rows_of(at), :] = inverse
            for k in range(FOLD):
                part, cols = flat[k * FOLD : (k + 1) * FOLD], slice(k * FOLDW, (k + 1) * FOLDW)
                pool_raw[rows_of(at), cols] = part.astype(BF)
                pool[rows_of(at), cols] = (part * inverse * gain[:, cols]).astype(BF)

        here = pl.ds(chunk * CROWS, CROWS)
        pool_scores[chunk, :, 0:CROWS] = matmul_t(query_embed[...], pool[here, :]) * SCALE
        pool_turned[chunk, :, 0:PAD] = matmul_t(pool[here, :], query_embed[...]) * SCALE

    live = [ask[:, c * 128 : c * 128 + CROWS] > 0 for c in range(CHUNKS)]
    masked = [
        jnp.where(live[c], pool_scores[c, :, 0:CROWS], -jnp.inf) for c in range(CHUNKS)
    ]
    main, rest = main_scores[...], rest_scores[...]
    peak = jnp.maximum(
        jnp.max(main, axis=1, keepdims=True), jnp.max(rest, axis=1, keepdims=True)
    )
    for c in range(CHUNKS):
        peak = jnp.maximum(peak, jnp.max(masked[c], axis=1, keepdims=True))
    added = jnp.sum(jnp.exp(main - peak), axis=1, keepdims=True)
    added = added + jnp.sum(jnp.exp(rest - peak), axis=1, keepdims=True)
    for c in range(CHUNKS):
        added = added + jnp.sum(jnp.exp(masked[c] - peak), axis=1, keepdims=True)
    total = peak + jnp.log(added)
    square = iota((PAD, 128), 0) == iota((PAD, 128), 1)
    total_row = jnp.sum(jnp.where(square, total, 0.0), axis=0, keepdims=True)

    give = Swap(me, term_stage, term_landed, term_send, term_recv, False)
    q_steps = [
        lambda: qs.relay(0),
        lambda: qs.relay(1),
        lambda: qs.relay(4),
        lambda: qs.pass_near(),
    ]
    for step in range(CHUNKS):
        chunk = CHUNKS - 1 - step
        column = to_column(ask[:, chunk * 128 : (chunk + 1) * 128], CROWS)
        turned = jnp.exp(pool_turned[chunk, :, 0:PAD] - total_row[:, 0:PAD])
        turned = jnp.where(column > 0, turned, 0.0).astype(BF)
        fold_rows(turned, query_embed, SCALE, swap, work, term_stage, terms, chunk)
        give.start(chunk, 0)
        give.start(chunk, 1)
        if step == 0:
            total_out[...] = jnp.concatenate(
                [
                    jnp.sum(jnp.where(main_hit, total, 0.0), axis=0, keepdims=True),
                    jnp.sum(jnp.where(rest_hit, total, 0.0), axis=0, keepdims=True),
                ],
                axis=1,
            )
            totals[blk] = total_out[...]
            total_copies = [
                remote(
                    total_out, totals.at[blk], total_send.at[d], total_recv.at[d],
                    blk=(blk + d) % NBLK,
                )
                for d in range(1, NBLK)
            ]
            for copy in total_copies:
                copy.start()
        q_steps[step]()
    term_landed[0:SLOTS] = term_stage[0:SLOTS]

    gain_sum[...] = jnp.zeros_like(gain_sum)
    main = jnp.exp(main - total) - jnp.where(main_hit, 1.0, 0.0)
    rest = jnp.where(rest_valid, jnp.exp(rest - total), 0.0) - jnp.where(rest_hit, 1.0, 0.0)
    coeffs = [jnp.exp(masked[c] - total).astype(BF) for c in range(CHUNKS)]

    def from_pool(cols):
        found = matmul(coeffs[0], pool[0:CROWS, cols])
        for c in range(1, CHUNKS):
            found = found + matmul(coeffs[c], pool[c * CROWS : (c + 1) * CROWS, cols])
        return found

    pair_grads(main, rest, phead, ptail, query_up, from_pool)
    norm_backward(query, query_inv, gain, query_up, query_grad, gain_sum)

    @pl.loop(0, POOL // FOLD)
    def _(g):
        at = rows_of(g * FOLD)
        gain_sum[...] += terms[at, :].astype(F32) * (pool_raw[at, :].astype(F32) * pool_inv[at, :])

    positive = jnp.sum(jnp.where(main_hit, main_scores[...], 0.0), axis=1, keepdims=True)
    positive = positive + jnp.sum(jnp.where(rest_hit, rest_scores[...], 0.0), axis=1, keepdims=True)
    loss = jnp.where(iota((PAD, 128), 0) < ROWS, total - positive, 0.0)
    loss = jnp.sum(loss, axis=0, keepdims=True)

    qs.pass_far()
    qs.finish()
    for copy in total_copies:
        copy.wait()
    lane_totals = totals[0]
    for b in range(1, NBLK):
        lane_totals = lane_totals + totals[b]
    main, rest = pair_scores(passage_embed, qhead, qtail)
    main = jnp.exp(main - lane_totals[:, :HEADS]) - jnp.where(main_hit, 1.0, 0.0)
    rest = jnp.exp(rest - lane_totals[:, HEADS:]) - jnp.where(rest_hit, 1.0, 0.0)
    rest = jnp.where(rest_valid, rest, 0.0)
    pair_grads(main, rest, qhead, qtail, passage_up, None)
    norm_backward(passage, passage_inv, gain, passage_up, None, gain_sum)

    run[0, :, 0:WIDTH] = jnp.sum(gain_sum[...], axis=0, keepdims=True)
    run[0, :, WIDTH:GAINS] = loss
    where = [
        lambda d: {"blk": (blk + d) % NBLK},
        lambda d: {"group": ((z + d) % NZ) * PLANE + plane},
        lambda d: {"group": z * PLANE + (plane + d) % PLANE},
    ]
    slots = (blk, z, plane)

    def sum_copies(level):
        return [
            remote(
                run.at[level], held.at[level, slots[level]],
                sum_send.at[level, d], sum_recv.at[level, d], **where[level](d),
            )
            for d in range(1, 8)
        ]

    def sum_start(level):
        held[level, slots[level]] = run[level]
        for copy in sum_copies(level):
            copy.start()

    def sum_end(level):
        for copy in sum_copies(level):
            copy.wait()
        got = held[level, 0]
        for d in range(1, 8):
            got = got + held[level, d]
        if level < 2:
            run[level + 1] = got
        else:
            sums[...] = got

    sum_start(0)
    for step in range(CHUNKS):
        chunk = CHUNKS - 1 - step
        give.arrived(chunk)

        @pl.loop(0, CROWS // FOLD)
        def _(g):
            at = chunk * CROWS + g * FOLD
            tile = term_landed[pl.ds(at, FOLD)].reshape(FOLDW, FOLDW)
            flat = matmul(swap[...], tile).astype(BF)
            for k in range(FOLD):
                terms[rows_of(at), k * FOLDW : (k + 1) * FOLDW] = flat[k * FOLD : (k + 1) * FOLD]

        if step == 1:
            sum_end(0)
            sum_start(1)
        if step == 3:
            sum_end(1)
            sum_start(2)

    names = [
        jnp.where(iota((PAD, CROWS), 0) + 1 == wanted[:, c * 128 : c * 128 + CROWS], 1.0, 0.0).astype(BF)
        for c in range(CHUNKS)
    ]

    @pl.loop(0, WIDTH // STRIP)
    def _(step):
        cols = pl.ds(pl.multiple_of(step * STRIP, STRIP), STRIP)
        found = passage_up[:, cols]
        for c in range(CHUNKS):
            found = found + matmul(names[c], terms[c * CROWS : (c + 1) * CROWS, cols])
        passage_up[:, cols] = found

    norm_backward(passage, passage_inv, gain, passage_up, passage_grad, None)
    sum_end(2)
    ps.sent()
    qs.sent()
    rows.sent()
    give.sent()


def requests(me, negative_owner, negative_row):
    entries = negative_owner.size
    turn = turn_of(me, negative_owner.reshape(entries))
    at = jnp.arange(entries, dtype=I32)
    rank = jnp.sum(
        jnp.where((turn[:, None] == turn[None, :]) & (at[None, :] < at[:, None]), 1, 0), axis=1
    )
    lane = (turn // 16) * 128 + (turn % 16) * SLOTS + rank
    hit = lane[:, None] == jnp.arange(LANES, dtype=I32)[None, :]
    return jnp.sum(jnp.where(hit, negative_row.reshape(entries)[:, None] + 1, 0), axis=0)[None, :]


def local(query_states, passage_states, norm_gain, negative_owner, negative_row):
    ask = requests(lax.axis_index("group"), negative_owner, negative_row)
    more = ((0, PAD - ROWS), (0, 0))
    vmem = pl.BlockSpec(memory_space=pltpu.VMEM)
    dma = pltpu.SemaphoreType.DMA
    query_grad, passage_grad, sums = pl.pallas_call(
        kernel,
        out_shape=(
            jax.ShapeDtypeStruct((PAD, WIDTH), F32),
            jax.ShapeDtypeStruct((PAD, WIDTH), F32),
            jax.ShapeDtypeStruct((1, GAINS), F32),
        ),
        in_specs=[vmem] * 4,
        out_specs=(vmem,) * 3,
        scratch_shapes=[
            pltpu.VMEM((PAD, WIDTH), BF),
            pltpu.VMEM((PAD, WIDTH), BF),
            pltpu.VMEM((PAD, 1), F32),
            pltpu.VMEM((PAD, 1), F32),
            pltpu.VMEM((FOLDW, FOLDW), BF),
            pltpu.VMEM((NBLK, HEAD, WIDTH), BF),
            pltpu.VMEM((NBLK, FOLD, TAILW), BF),
            pltpu.VMEM((NBLK, HEAD, WIDTH), BF),
            pltpu.VMEM((NBLK, FOLD, TAILW), BF),
            pltpu.VMEM((NGROUP, 1, LANES), I32),
            pltpu.VMEM((CROWS // FOLD, FOLDW, FOLDW), BF),
            pltpu.VMEM((POOL, FOLD, FOLDW), BF),
            pltpu.VMEM((POOL, FOLD, FOLDW), BF),
            pltpu.VMEM((POOL, WIDTH), BF),
            pltpu.VMEM((POOL, WIDTH), BF),
            pltpu.VMEM((POOL, 1), F32),
            pltpu.VMEM((CHUNKS, PAD, 128), F32),
            pltpu.VMEM((CHUNKS, CROWS, 128), F32),
            pltpu.VMEM((POOL, WIDTH), BF),
            pltpu.VMEM((POOL, FOLD, FOLDW), BF),
            pltpu.VMEM((POOL, FOLD, FOLDW), BF),
            pltpu.VMEM((PAD, HEADS), F32),
            pltpu.VMEM((PAD, TAILS), F32),
            pltpu.VMEM((1, HEADS + TAILS), F32),
            pltpu.VMEM((NBLK, 1, HEADS + TAILS), F32),
            pltpu.VMEM((PAD, WIDTH), F32),
            pltpu.VMEM((PAD, WIDTH), F32),
            pltpu.VMEM((FOLD, WIDTH), F32),
            pltpu.VMEM((3, 8, 1, GAINS), F32),
            pltpu.VMEM((3, 1, GAINS), F32),
            *[dma((NGROUP,))] * 6,
            *[dma((8, 5))] * 4,
            *[dma((NBLK,))] * 2,
            *[dma((3, 8))] * 2,
        ],
        compiler_params=pltpu.CompilerParams(
            collective_id=0, has_side_effects=True, vmem_limit_bytes=VMEM_LIMIT
        ),
    )(jnp.pad(query_states, more), jnp.pad(passage_states, more), norm_gain[None, :], ask)
    loss = sums[0, WIDTH] / (ROWS * NBLK * NGROUP)
    return (query_grad[:ROWS], passage_grad[:ROWS], sums[0, :WIDTH], loss)

def solution(mesh):
    return jax.shard_map(
        local,
        mesh=mesh,
        in_specs=(
            P(("blk", "group"), None),
            P(("blk", "group"), None),
            P(),
            P(("blk", "group"), None),
            P(("blk", "group"), None),
        ),
        out_specs=(P(("blk", "group"), None), P(("blk", "group"), None), P(), P()),
        check_vma=False,
    )
```

```python
import math

import jax
import jax.numpy as jnp
from jax import lax
from jax.experimental import pallas as pl
from jax.experimental.pallas import tpu as pltpu
from jax.sharding import PartitionSpec as P

EPSILON = 1e-05
MESH = pl.DeviceIdType.MESH
NZ, NY, NX = 8, 2, 4
NGROUP = NZ * NY * NX
NPOS, NCORE = 4, 2
NBLK = NPOS * NCORE
ROWS, WIDTH = 72, 4096
PAD = 80
SLOTS = 5
POOL = NGROUP * SLOTS
CHUNKS = NZ // 2
CROWS = POOL // CHUNKS
PLANE = NY * NX
LANES = CHUNKS * 128
FOLD, FOLDW = 16, 256
HEAD, TAILW = 64, 2048
HEADS, TAILS = NBLK * HEAD, NBLK * FOLD
STRIP = 512
DZ = (0, 1, 7, 4, 2, 6, 3, 5)
ORDER = (1, 0, 3, 2)
SCALE = 4.0 / math.sqrt(WIDTH)
GAINS = WIDTH + 128
VMEM_LIMIT = 60 * 1024 * 1024
BF, F32, I32 = jnp.bfloat16, jnp.float32, jnp.int32


class Peers:
    def __init__(self, me, back=False):
        self.z, self.y, self.x = me // PLANE, (me // NX) % NY, me % NX
        self.back = back

    def plane(self, dy, dx):
        x = self.x + NX - dx if self.back else self.x + dx
        return ((self.y + dy) % NY) * NX + x % NX

    def level(self, place):
        dz = DZ[place]
        return (self.z + NZ - dz if self.back else self.z + dz) % NZ

    def all(self, act):
        levels = [self.level(place) for place in range(NZ)]

        @pl.loop(0, NX)
        def _(dx):
            for dy in range(NY):
                plane = self.plane(dy, dx)
                for place in range(NZ):
                    turn, other = (dy * NZ + place) * NX + dx, levels[place] * PLANE + plane
                    if dy > 0 or place > 0:
                        act(turn, other)
                    else:

                        @pl.when(dx > 0)
                        def _():
                            act(turn, other)


def turn_of(me, other):
    dz = (other // (NY * NX) - me // (NY * NX)) % NZ
    dy = ((other // NX) % NY - (me // NX) % NY) % NY
    dx = (other % NX - me % NX) % NX
    place = sum(jnp.where(dz == step, at, 0) for at, step in enumerate(DZ))
    return (dy * NZ + place) * NX + dx


def remote(src, dst, send, recv, **where):
    return pltpu.make_async_remote_copy(
        src_ref=src, dst_ref=dst, send_sem=send, recv_sem=recv, device_id=where, device_id_type=MESH
    )


class Spread:
    def __init__(self, blk, head, tail, send, recv):
        pos, core = blk // NCORE, blk % NCORE
        self.own = blk
        self.right = ((pos + 1) % NPOS) * NCORE + core
        self.left = ((pos + 3) % NPOS) * NCORE + core
        self.far = ((pos + 2) % NPOS) * NCORE + core
        self.twin = pos * NCORE + 1 - core
        self.head, self.tail, self.send, self.recv = head, tail, send, recv
        self.started = []

    def copy(self, kind, slot, piece, target):
        if piece < 4 and kind in (0, 1, 3, 5):
            ref = self.head.at[slot, pl.ds(piece * FOLD, FOLD)]
        elif piece < 4:
            ref = self.head.at[slot]
        elif kind in (3, 5):
            ref = self.tail.at[slot, :, pl.ds((kind // 5) * (TAILW // 2), TAILW // 2)]
        else:
            ref = self.tail.at[slot]
        sems = self.send.at[kind, piece], self.recv.at[kind, piece]
        return remote(ref, ref, *sems, blk=target)

    def start(self, kind, slot, piece, target):
        copy = self.copy(kind, slot, piece, target)
        copy.start()
        self.started.append(copy)

    def arrived(self, kind, slot, piece):
        self.copy(kind, slot, piece, self.own).wait_recv()

    def hop(self, *pieces):
        for piece in pieces:
            self.start(0, self.own, piece, self.right)
            self.start(1, self.own, (2, 3, 0, 1, 4)[piece], self.left)

    def over(self, kind, slot):
        self.start(kind, slot, 0, self.twin)
        self.start(kind, slot, 4, self.twin)

    def relay(self, *pieces):
        for piece in pieces:
            self.arrived(0, self.left, piece)
            self.start(3, self.left, piece, self.right)
            other = (2, 3, 0, 1, 4)[piece]
            self.arrived(1, self.right, other)
            self.start(5, self.right, other, self.left)

    def pass_near(self):
        self.arrived(0, self.left, 2)
        self.arrived(0, self.left, 3)
        self.over(4, self.left)
        self.arrived(1, self.right, 0)
        self.arrived(1, self.right, 1)
        self.over(6, self.right)

    def pass_far(self):
        for piece in (0, 1, 4):
            self.arrived(3, self.far, piece)
        for piece in (2, 3, 4):
            self.arrived(5, self.far, piece)
        self.over(7, self.far)

    def finish(self):
        for kind in (2, 4, 6, 7):
            self.arrived(kind, self.twin, 0)
            self.arrived(kind, self.twin, 4)

    def sent(self):
        for copy in self.started:
            copy.wait_send()


class Swap:
    def __init__(self, peers, src, dst, send, recv):
        self.peers, self.src, self.dst, self.send, self.recv = peers, src, dst, send, recv

    def message(self, turn, other):
        rows = pl.ds(turn * SLOTS, SLOTS)
        return remote(
            self.src.at[rows], self.dst.at[rows], self.send.at[turn], self.recv.at[turn], group=other
        )

    def start(self, chunk, half):
        dy = chunk // 2

        @pl.loop(half * (NX // 2), (half + 1) * (NX // 2))
        def _(dx):
            plane = self.peers.plane(dy, dx)
            for place in range((chunk % 2) * (NZ // 2), (chunk % 2 + 1) * (NZ // 2)):
                turn = (dy * NZ + place) * NX + dx
                copy = self.message(turn, self.peers.level(place) * PLANE + plane)
                if dy > 0 or place > 0:
                    copy.start()
                else:

                    @pl.when(dx > 0)
                    def _():
                        copy.start()

    def arrived(self, chunk):
        @pl.loop(max(1, 2 * PLANE * chunk), 2 * PLANE * (chunk + 1))
        def _(turn):
            self.message(turn, 0).wait_recv()

    def sent(self):
        @pl.loop(1, NGROUP)
        def _(turn):
            self.message(turn, 0).wait_send()


def iota(shape, dim):
    return lax.broadcasted_iota(I32, shape, dim)


def rows_of(start, count=FOLD):
    return pl.ds(pl.multiple_of(start, FOLD), count)


def to_column(row, count):
    same = iota((count, 128), 0) == iota((count, 128), 1)
    return jnp.sum(jnp.where(same, jnp.broadcast_to(row, (count, 128)), 0), axis=1, keepdims=True)


def matmul(left, right):
    return jnp.dot(left, right, preferred_element_type=F32)


def matmul_t(left, right):
    return lax.dot_general(left, right, (((1,), (1,)), ((), ())), preferred_element_type=F32)


def embed(states, gain, out, inverses):
    @pl.loop(0, PAD // FOLD)
    def _(step):
        at = rows_of(step * FOLD)
        values = states[at, :].astype(F32)
        inverse = lax.rsqrt(jnp.mean(values * values, axis=-1, keepdims=True) + EPSILON)
        inverses[at, :] = inverse
        out[at, :] = (values * inverse * gain[...]).astype(BF)


def place_own(blk, embedded, head, tail):
    head[blk] = embedded[0:HEAD, :]
    last = embedded[HEAD:PAD, :]
    last = last.astype(F32)[0 : ROWS - HEAD]
    tail[blk] = jnp.concatenate([last[:, :TAILW], last[:, TAILW:]], axis=0).astype(BF)


def fold_rows(left, right, factor, swap, work, stage, flat, chunk):
    first = chunk * CROWS

    @pl.loop(0, FOLD)
    def _(k):
        cols = pl.ds(pl.multiple_of(k * FOLDW, FOLDW), FOLDW)
        found = matmul(left, right[:, cols])
        if factor is not None:
            found = factor * found
        found = found.astype(BF)
        if flat is not None:
            flat[rows_of(first, CROWS), cols] = found
        work[:, rows_of(k * FOLD), :] = found.reshape(CROWS // FOLD, FOLD, FOLDW)

    for g in range(CROWS // FOLD):
        folded = matmul(swap[...], work[g]).astype(BF)
        stage[pl.ds(first + g * FOLD, FOLD)] = folded.reshape(FOLD, FOLD, FOLDW)


def pair_scores(embedded, head, tail):
    main = matmul_t(embedded[...], head[...].reshape(HEADS, WIDTH)) * SCALE
    folded = tail[...].reshape(TAILS, TAILW)
    low = matmul_t(embedded[:, :TAILW], folded)
    high = matmul_t(embedded[:, TAILW:], folded)
    return main, (low + pltpu.roll(high, TAILS - (ROWS - HEAD), 1)) * SCALE


def pair_masks(blk):
    row, lane = iota((PAD, HEADS), 0), iota((PAD, HEADS), 1)
    main = (row < HEAD) & (lane == blk * HEAD + row)
    row, lane = iota((PAD, TAILS), 0), iota((PAD, TAILS), 1)
    valid = (lane // (ROWS - HEAD)) % 2 == 0
    rest = (row >= HEAD) & (row < ROWS) & (lane == blk * FOLD + row - HEAD)
    return main, rest, valid


def pair_grads(main, rest, head, tail, out, extra):
    low = rest.astype(BF)
    high = pltpu.roll(rest, ROWS - HEAD, 1).astype(BF)
    main = main.astype(BF)
    for part, coeff in enumerate((low, high)):

        @pl.loop(0, TAILW // STRIP)
        def _(step):
            near = pl.ds(pl.multiple_of(step * STRIP, STRIP), STRIP)
            cols = pl.ds(pl.multiple_of(part * TAILW + step * STRIP, STRIP), STRIP)
            found = matmul(main, head[:, :, cols].reshape(HEADS, STRIP))
            found = found + matmul(coeff, tail[:, :, near].reshape(TAILS, STRIP))
            if extra is not None:
                found = found + extra(cols)
            out[:, cols] = SCALE * found


def norm_backward(states, inverses, gain, upstream, out, gain_sum):
    def rows(at, count):
        values, inverse, given = states[at, :].astype(F32), inverses[at, :], upstream[at, :]
        if out is not None:
            scaled = gain[...] * given
            inner = jnp.sum(scaled * values, axis=-1, keepdims=True)
            found = scaled * inverse - values * inverse**3 * inner / WIDTH
            out[pl.ds(at.start, count), :] = found[:count]
        if gain_sum is not None:
            gain_sum[...] += given * values * inverse

    @pl.loop(0, HEAD // FOLD)
    def _(step):
        rows(rows_of(step * FOLD), FOLD)

    rows(pl.ds(HEAD, FOLD), ROWS - HEAD)


def requests(me, owner, row, ask):
    turns = [turn_of(me, owner[:, k : k + 1]) for k in range(owner.shape[1])]
    down, across = iota((ROWS, 128), 0), iota((ROWS, 128), 1)
    lines = [jnp.sum(jnp.where(down == across, turn, 0), axis=0, keepdims=True) for turn in turns]
    found = jnp.zeros((1, LANES), I32)
    for k, turn in enumerate(turns):
        earlier = jnp.where((turn == lines[k]) & (across < down), 1, 0)
        for line in lines[:k]:
            earlier = earlier + jnp.where((turn == line) & (across < ROWS), 1, 0)
        rank = jnp.sum(earlier, axis=1, keepdims=True)
        lane = (turn // 16) * 128 + (turn % 16) * SLOTS + rank
        hit = lane == iota((ROWS, LANES), 1)
        found = found + jnp.sum(jnp.where(hit, row[:, k : k + 1] + 1, 0), axis=0, keepdims=True)
    ask[...] = found


def kernel(
    both, gain, owner, row_asked,
    query_grad, passage_grad, sums,
    query, passage, ask, query_embed, passage_embed, query_inv, passage_inv, swap,
    phead, ptail, qhead, qtail,
    asked, mine, work, stage, landed, pool, pool_raw, pool_inv, pool_scores, pool_turned,
    terms, term_stage, term_landed,
    main_scores, rest_scores, total_out, totals, query_up, passage_up, gain_sum, held, run,
    ask_send, ask_recv, row_send, row_recv, term_send, term_recv,
    p_send, p_recv, q_send, q_recv, total_send, total_recv, sum_send, sum_recv,
):
    me, blk = lax.axis_index("group"), lax.axis_index("blk")
    z, plane = me // PLANE, me % PLANE
    barrier = pltpu.get_barrier_semaphore()

    there, back = Peers(me), Peers(me, True)

    there.all(
        lambda turn, other: pl.semaphore_signal(
            barrier, inc=1, device_id={"group": other}, device_id_type=MESH
        )
    )

    for d in range(1, NBLK):
        pl.semaphore_signal(barrier, inc=1, device_id={"blk": (blk + d) % NBLK}, device_id_type=MESH)

    requests(me, owner, row_asked, ask)
    asked[0] = ask[...]
    query[0:HEAD] = both[0:HEAD]
    passage[0:HEAD] = both[HEAD : 2 * HEAD]
    last, none = both[2 * HEAD : 2 * ROWS].astype(F32), jnp.zeros((PAD - ROWS, WIDTH), F32)
    query[HEAD:PAD] = jnp.concatenate([last[: ROWS - HEAD], none], axis=0).astype(BF)
    passage[HEAD:PAD] = jnp.concatenate([last[ROWS - HEAD :], none], axis=0).astype(BF)
    embed(passage, gain, passage_embed, passage_inv)
    place_own(blk, passage_embed, phead, ptail)
    row, col = iota((FOLDW, FOLDW), 0), iota((FOLDW, FOLDW), 1)
    same = (row // FOLD == col % FOLD) & (row % FOLD == col // FOLD)
    swap[...] = jnp.where(same, 1.0, 0.0).astype(BF)
    turns = iota((NGROUP, 1, LANES), 0)
    past = iota((NGROUP, 1, LANES), 2) - (turns // 16) * 128 - (turns % 16) * SLOTS
    mine[...] = jnp.where((past >= 0) & (past < SLOTS), 1, 0)
    pl.semaphore_wait(barrier, NGROUP - 1 + NBLK - 1)

    def asking(turn, other):
        return remote(ask, asked.at[turn], ask_send.at[turn], ask_recv.at[turn], group=other)

    there.all(lambda turn, other: asking(turn, other).start())

    ps = Spread(blk, phead, ptail, p_send, p_recv)
    qs = Spread(blk, qhead, qtail, q_send, q_recv)
    ps.hop(0, 1)
    embed(query, gain, query_embed, query_inv)
    place_own(blk, query_embed, qhead, qtail)

    @pl.loop(1, NGROUP)
    def _(turn):
        asking(turn, 0).wait()

    wanted = jnp.sum(asked[...] * mine[...], axis=0)

    rows = Swap(back, stage, landed, row_send, row_recv)
    spread_steps = [
        lambda: ps.hop(4),
        lambda: ps.hop(2),
        lambda: ps.hop(3),
        lambda: (ps.over(2, blk), ps.relay(0)),
        lambda: ps.relay(1),
        lambda: ps.relay(4),
        lambda: ps.pass_near(),
        lambda: None,
    ]
    for step in range(CHUNKS):
        chunk = ORDER[step]
        column = to_column(wanted[:, chunk * 128 : (chunk + 1) * 128], CROWS)
        pick = jnp.where(column - 1 == iota((CROWS, PAD), 1), 1.0, 0.0).astype(BF)
        fold_rows(pick, passage, None, swap, work, stage, None, chunk)
        for half in range(2):
            rows.start(chunk, half)
            spread_steps[2 * step + half]()
    landed[0:SLOTS] = stage[0:SLOTS]
    qs.hop(0, 1, 4)
    ps.pass_far()
    ps.finish()

    main_hit, rest_hit, rest_valid = pair_masks(blk)
    main, rest = pair_scores(query_embed, phead, ptail)
    main_scores[...] = main
    rest_scores[...] = jnp.where(rest_valid, rest, -jnp.inf)

    for step in range(CHUNKS):
        chunk = ORDER[step]
        rows.arrived(chunk)

        @pl.loop(0, CROWS // FOLD)
        def _(g):
            at = chunk * CROWS + g * FOLD
            tile = landed[pl.ds(at, FOLD)].reshape(FOLDW, FOLDW)
            flat = matmul(swap[...], tile)
            square = jnp.zeros((FOLD, FOLDW), F32)
            for k in range(FOLD):
                part = flat[k * FOLD : (k + 1) * FOLD]
                square = square + part * part
            inverse = lax.rsqrt(jnp.sum(square, axis=1, keepdims=True) / WIDTH + EPSILON)
            pool_inv[rows_of(at), :] = inverse
            for k in range(FOLD):
                part, cols = flat[k * FOLD : (k + 1) * FOLD], slice(k * FOLDW, (k + 1) * FOLDW)
                pool_raw[rows_of(at), cols] = part.astype(BF)
                pool[rows_of(at), cols] = (part * inverse * gain[:, cols]).astype(BF)

        here = pl.ds(chunk * CROWS, CROWS)
        pool_scores[chunk, :, 0:CROWS] = matmul_t(query_embed[...], pool[here, :]) * SCALE
        pool_turned[chunk, :, 0:PAD] = matmul_t(pool[here, :], query_embed[...]) * SCALE

    live = [ask[:, c * 128 : c * 128 + CROWS] > 0 for c in range(CHUNKS)]
    masked = [
        jnp.where(live[c], pool_scores[c, :, 0:CROWS], -jnp.inf) for c in range(CHUNKS)
    ]
    main, rest = main_scores[...], rest_scores[...]
    peak = jnp.maximum(
        jnp.max(main, axis=1, keepdims=True), jnp.max(rest, axis=1, keepdims=True)
    )
    for c in range(CHUNKS):
        peak = jnp.maximum(peak, jnp.max(masked[c], axis=1, keepdims=True))
    added = jnp.sum(jnp.exp(main - peak), axis=1, keepdims=True)
    added = added + jnp.sum(jnp.exp(rest - peak), axis=1, keepdims=True)
    for c in range(CHUNKS):
        added = added + jnp.sum(jnp.exp(masked[c] - peak), axis=1, keepdims=True)
    total = peak + jnp.log(added)
    square = iota((PAD, 128), 0) == iota((PAD, 128), 1)
    total_row = jnp.sum(jnp.where(square, total, 0.0), axis=0, keepdims=True)

    give = Swap(there, term_stage, term_landed, term_send, term_recv)
    q_steps = [
        lambda: qs.relay(0),
        lambda: qs.relay(4),
        lambda: qs.pass_near(),
        lambda: qs.pass_far(),
    ]
    for step in range(CHUNKS):
        chunk = ORDER[step]
        column = to_column(ask[:, chunk * 128 : (chunk + 1) * 128], CROWS)
        turned = jnp.exp(pool_turned[chunk, :, 0:PAD] - total_row[:, 0:PAD])
        turned = jnp.where(column > 0, turned, 0.0).astype(BF)
        fold_rows(turned, query_embed, SCALE, swap, work, term_stage, terms, chunk)
        give.start(chunk, 0)
        if step == 0:
            qs.hop(2, 3)
            qs.over(2, blk)
        if step == 1:
            qs.relay(1)
        give.start(chunk, 1)
        if step == 0:
            total_out[...] = jnp.concatenate(
                [
                    jnp.sum(jnp.where(main_hit, total, 0.0), axis=0, keepdims=True),
                    jnp.sum(jnp.where(rest_hit, total, 0.0), axis=0, keepdims=True),
                ],
                axis=1,
            )
            totals[blk] = total_out[...]
            total_copies = [
                remote(
                    total_out, totals.at[blk], total_send.at[d], total_recv.at[d],
                    blk=(blk + d) % NBLK,
                )
                for d in range(1, NBLK)
            ]
            for copy in total_copies:
                copy.start()
        q_steps[step]()
    term_landed[0:SLOTS] = term_stage[0:SLOTS]

    gain_sum[...] = jnp.zeros_like(gain_sum)
    main = jnp.exp(main - total) - jnp.where(main_hit, 1.0, 0.0)
    rest = jnp.where(rest_valid, jnp.exp(rest - total), 0.0) - jnp.where(rest_hit, 1.0, 0.0)
    coeffs = [jnp.exp(masked[c] - total).astype(BF) for c in range(CHUNKS)]

    def from_pool(cols):
        found = matmul(coeffs[0], pool[0:CROWS, cols])
        for c in range(1, CHUNKS):
            found = found + matmul(coeffs[c], pool[c * CROWS : (c + 1) * CROWS, cols])
        return found

    pair_grads(main, rest, phead, ptail, query_up, from_pool)
    norm_backward(query, query_inv, gain, query_up, query_grad, gain_sum)

    @pl.loop(0, POOL // FOLD)
    def _(g):
        at = rows_of(g * FOLD)
        gain_sum[...] += terms[at, :].astype(F32) * (pool_raw[at, :].astype(F32) * pool_inv[at, :])

    positive = jnp.sum(jnp.where(main_hit, main_scores[...], 0.0), axis=1, keepdims=True)
    positive = positive + jnp.sum(jnp.where(rest_hit, rest_scores[...], 0.0), axis=1, keepdims=True)
    loss = jnp.where(iota((PAD, 128), 0) < ROWS, total - positive, 0.0)
    loss = jnp.sum(loss, axis=0, keepdims=True)

    qs.finish()
    for copy in total_copies:
        copy.wait()
    lane_totals = totals[0]
    for b in range(1, NBLK):
        lane_totals = lane_totals + totals[b]
    main, rest = pair_scores(passage_embed, qhead, qtail)
    main = jnp.exp(main - lane_totals[:, :HEADS]) - jnp.where(main_hit, 1.0, 0.0)
    rest = jnp.exp(rest - lane_totals[:, HEADS:]) - jnp.where(rest_hit, 1.0, 0.0)
    rest = jnp.where(rest_valid, rest, 0.0)
    pair_grads(main, rest, qhead, qtail, passage_up, None)
    norm_backward(passage, passage_inv, gain, passage_up, None, gain_sum)

    run[0, :, 0:WIDTH] = jnp.sum(gain_sum[...], axis=0, keepdims=True)
    run[0, :, WIDTH:GAINS] = loss
    where = [
        lambda d: {"blk": (blk + d) % NBLK},
        lambda d: {"group": ((z + d) % NZ) * PLANE + plane},
        lambda d: {"group": z * PLANE + (plane + d) % PLANE},
    ]
    slots = (blk, z, plane)

    def sum_copies(level):
        return [
            remote(
                run.at[level], held.at[level, slots[level]],
                sum_send.at[level, d], sum_recv.at[level, d], **where[level](d),
            )
            for d in range(1, 8)
        ]

    def sum_start(level):
        held[level, slots[level]] = run[level]
        for copy in sum_copies(level):
            copy.start()

    def sum_end(level):
        for copy in sum_copies(level):
            copy.wait()
        got = held[level, 0]
        for d in range(1, 8):
            got = got + held[level, d]
        if level < 2:
            run[level + 1] = got
        else:
            sums[...] = got

    sum_start(0)
    for step in range(CHUNKS):
        chunk = ORDER[step]
        give.arrived(chunk)
        lanes = slice(chunk * 128, chunk * 128 + CROWS)
        names = jnp.where(iota((PAD, CROWS), 0) + 1 == wanted[:, lanes], 1.0, 0.0).astype(BF)

        @pl.loop(0, CROWS // FOLD)
        def _(g):
            at = chunk * CROWS + g * FOLD
            tile = term_landed[pl.ds(at, FOLD)].reshape(FOLDW, FOLDW)
            flat = matmul(swap[...], tile).astype(BF)
            for k in range(FOLD):
                terms[rows_of(at), k * FOLDW : (k + 1) * FOLDW] = flat[k * FOLD : (k + 1) * FOLD]

        if step == 1:
            sum_end(0)
            sum_start(1)
        if step == 2:
            sum_end(1)
            sum_start(2)

    names = [
        jnp.where(iota((PAD, CROWS), 0) + 1 == wanted[:, c * 128 : c * 128 + CROWS], 1.0, 0.0).astype(BF)
        for c in range(CHUNKS)
    ]

    @pl.loop(0, WIDTH // STRIP)
    def _(step):
        cols = pl.ds(pl.multiple_of(step * STRIP, STRIP), STRIP)
        found = passage_up[:, cols]
        for c in range(CHUNKS):
            found = found + matmul(names[c], terms[c * CROWS : (c + 1) * CROWS, cols])
        passage_up[:, cols] = found

    norm_backward(passage, passage_inv, gain, passage_up, passage_grad, None)
    sum_end(2)
    ps.sent()
    qs.sent()
    rows.sent()
    give.sent()


def local(query_states, passage_states, norm_gain, negative_owner, negative_row):
    both = jnp.concatenate(
        [
            query_states[:HEAD], passage_states[:HEAD],
            query_states[HEAD:], passage_states[HEAD:],
        ]
    )
    vmem = pl.BlockSpec(memory_space=pltpu.VMEM)
    dma = pltpu.SemaphoreType.DMA
    query_grad, passage_grad, sums = pl.pallas_call(
        kernel,
        out_shape=(
            jax.ShapeDtypeStruct((ROWS, WIDTH), F32),
            jax.ShapeDtypeStruct((ROWS, WIDTH), F32),
            jax.ShapeDtypeStruct((1, GAINS), F32),
        ),
        in_specs=[vmem] * 4,
        out_specs=(vmem,) * 3,
        scratch_shapes=[
            pltpu.VMEM((PAD, WIDTH), BF),
            pltpu.VMEM((PAD, WIDTH), BF),
            pltpu.VMEM((1, LANES), I32),
            pltpu.VMEM((PAD, WIDTH), BF),
            pltpu.VMEM((PAD, WIDTH), BF),
            pltpu.VMEM((PAD, 1), F32),
            pltpu.VMEM((PAD, 1), F32),
            pltpu.VMEM((FOLDW, FOLDW), BF),
            pltpu.VMEM((NBLK, HEAD, WIDTH), BF),
            pltpu.VMEM((NBLK, FOLD, TAILW), BF),
            pltpu.VMEM((NBLK, HEAD, WIDTH), BF),
            pltpu.VMEM((NBLK, FOLD, TAILW), BF),
            pltpu.VMEM((NGROUP, 1, LANES), I32),
            pltpu.VMEM((NGROUP, 1, LANES), I32),
            pltpu.VMEM((CROWS // FOLD, FOLDW, FOLDW), BF),
            pltpu.VMEM((POOL, FOLD, FOLDW), BF),
            pltpu.VMEM((POOL, FOLD, FOLDW), BF),
            pltpu.VMEM((POOL, WIDTH), BF),
            pltpu.VMEM((POOL, WIDTH), BF),
            pltpu.VMEM((POOL, 1), F32),
            pltpu.VMEM((CHUNKS, PAD, 128), F32),
            pltpu.VMEM((CHUNKS, CROWS, 128), F32),
            pltpu.VMEM((POOL, WIDTH), BF),
            pltpu.VMEM((POOL, FOLD, FOLDW), BF),
            pltpu.VMEM((POOL, FOLD, FOLDW), BF),
            pltpu.VMEM((PAD, HEADS), F32),
            pltpu.VMEM((PAD, TAILS), F32),
            pltpu.VMEM((1, HEADS + TAILS), F32),
            pltpu.VMEM((NBLK, 1, HEADS + TAILS), F32),
            pltpu.VMEM((PAD, WIDTH), F32),
            pltpu.VMEM((PAD, WIDTH), F32),
            pltpu.VMEM((FOLD, WIDTH), F32),
            pltpu.VMEM((3, 8, 1, GAINS), F32),
            pltpu.VMEM((3, 1, GAINS), F32),
            *[dma((NGROUP,))] * 6,
            *[dma((8, 5))] * 4,
            *[dma((NBLK,))] * 2,
            *[dma((3, 8))] * 2,
        ],
        compiler_params=pltpu.CompilerParams(
            collective_id=0, has_side_effects=True, vmem_limit_bytes=VMEM_LIMIT
        ),
    )(both, norm_gain[None, :], negative_owner, negative_row)
    loss = sums[0, WIDTH] / (ROWS * NBLK * NGROUP)
    return (query_grad, passage_grad, sums[0, :WIDTH], loss)

def solution(mesh):
    return jax.shard_map(
        local,
        mesh=mesh,
        in_specs=(
            P(("blk", "group"), None),
            P(("blk", "group"), None),
            P(),
            P(("blk", "group"), None),
            P(("blk", "group"), None),
        ),
        out_specs=(P(("blk", "group"), None), P(("blk", "group"), None), P(), P()),
        check_vma=False,
    )
```

```python
import math

import jax
import jax.numpy as jnp
from jax import lax
from jax.experimental import pallas as pl
from jax.experimental.pallas import tpu as pltpu
from jax.sharding import PartitionSpec as P

EPSILON = 1e-05
MESH = pl.DeviceIdType.MESH
NZ, NY, NX = 8, 2, 4
NGROUP = NZ * NY * NX
NPOS, NCORE = 4, 2
NBLK = NPOS * NCORE
ROWS, WIDTH = 72, 4096
PAD = 80
SLOTS = 5
POOL = NGROUP * SLOTS
CHUNKS = NZ // 2
CROWS = POOL // CHUNKS
PLANE = NY * NX
LANES = CHUNKS * 128
FOLD, FOLDW = 16, 256
HEAD, TAILW = 64, 2048
HEADS, TAILS = NBLK * HEAD, NBLK * FOLD
STRIP = 512
DZ = (0, 1, 7, 4, 2, 6, 3, 5)
ORDER = (1, 0, 3, 2)
SCALE = 4.0 / math.sqrt(WIDTH)
GAINS = WIDTH + 128
VMEM_LIMIT = 60 * 1024 * 1024
BF, F32, I32 = jnp.bfloat16, jnp.float32, jnp.int32


class Peers:
    def __init__(self, me, back=False):
        self.z, self.y, self.x = me // PLANE, (me // NX) % NY, me % NX
        self.back = back

    def plane(self, dy, dx):
        x = self.x + NX - dx if self.back else self.x + dx
        return ((self.y + dy) % NY) * NX + x % NX

    def level(self, place):
        dz = DZ[place]
        return (self.z + NZ - dz if self.back else self.z + dz) % NZ

    def all(self, act):
        levels = [self.level(place) for place in range(NZ)]

        @pl.loop(0, NX)
        def _(dx):
            for dy in range(NY):
                plane = self.plane(dy, dx)
                for place in range(NZ):
                    turn, other = (dy * NZ + place) * NX + dx, levels[place] * PLANE + plane
                    if dy > 0 or place > 0:
                        act(turn, other)
                    else:

                        @pl.when(dx > 0)
                        def _():
                            act(turn, other)


def turn_of(me, other):
    dz = (other // (NY * NX) - me // (NY * NX)) % NZ
    dy = ((other // NX) % NY - (me // NX) % NY) % NY
    dx = (other % NX - me % NX) % NX
    place = sum(jnp.where(dz == step, at, 0) for at, step in enumerate(DZ))
    return (dy * NZ + place) * NX + dx


def remote(src, dst, send, recv, **where):
    return pltpu.make_async_remote_copy(
        src_ref=src, dst_ref=dst, send_sem=send, recv_sem=recv, device_id=where, device_id_type=MESH
    )


class Spread:
    def __init__(self, blk, head, tail, send, recv):
        pos, core = blk // NCORE, blk % NCORE
        self.own = blk
        self.right = ((pos + 1) % NPOS) * NCORE + core
        self.left = ((pos + 3) % NPOS) * NCORE + core
        self.far = ((pos + 2) % NPOS) * NCORE + core
        self.twin = pos * NCORE + 1 - core
        self.head, self.tail, self.send, self.recv = head, tail, send, recv
        self.started = []

    def copy(self, kind, slot, piece, target):
        if piece < 4 and kind in (0, 1, 3, 5):
            ref = self.head.at[slot, pl.ds(piece * FOLD, FOLD)]
        elif piece < 4:
            ref = self.head.at[slot]
        elif kind in (3, 5):
            ref = self.tail.at[slot, :, pl.ds((kind // 5) * (TAILW // 2), TAILW // 2)]
        else:
            ref = self.tail.at[slot]
        sems = self.send.at[kind, piece], self.recv.at[kind, piece]
        return remote(ref, ref, *sems, blk=target)

    def start(self, kind, slot, piece, target):
        copy = self.copy(kind, slot, piece, target)
        copy.start()
        self.started.append(copy)

    def arrived(self, kind, slot, piece):
        self.copy(kind, slot, piece, self.own).wait_recv()

    def hop(self, *pieces):
        for piece in pieces:
            self.start(0, self.own, piece, self.right)
            self.start(1, self.own, (2, 3, 0, 1, 4)[piece], self.left)

    def over(self, kind, slot):
        self.start(kind, slot, 0, self.twin)
        self.start(kind, slot, 4, self.twin)

    def relay(self, *pieces):
        for piece in pieces:
            self.arrived(0, self.left, piece)
            self.start(3, self.left, piece, self.right)
            other = (2, 3, 0, 1, 4)[piece]
            self.arrived(1, self.right, other)
            self.start(5, self.right, other, self.left)

    def pass_near(self):
        self.arrived(0, self.left, 2)
        self.arrived(0, self.left, 3)
        self.over(4, self.left)
        self.arrived(1, self.right, 0)
        self.arrived(1, self.right, 1)
        self.over(6, self.right)

    def pass_far(self):
        for piece in (0, 1, 4):
            self.arrived(3, self.far, piece)
        for piece in (2, 3, 4):
            self.arrived(5, self.far, piece)
        self.over(7, self.far)

    def finish(self):
        for kind in (2, 4, 6, 7):
            self.arrived(kind, self.twin, 0)
            self.arrived(kind, self.twin, 4)

    def sent(self):
        for copy in self.started:
            copy.wait_send()


class Swap:
    def __init__(self, peers, src, dst, send, recv):
        self.peers, self.src, self.dst, self.send, self.recv = peers, src, dst, send, recv

    def message(self, turn, other):
        rows = pl.ds(turn * SLOTS, SLOTS)
        return remote(
            self.src.at[rows], self.dst.at[rows], self.send.at[turn], self.recv.at[turn], group=other
        )

    def start(self, chunk, half):
        dy = chunk // 2

        @pl.loop(half * (NX // 2), (half + 1) * (NX // 2))
        def _(dx):
            plane = self.peers.plane(dy, dx)
            for place in range((chunk % 2) * (NZ // 2), (chunk % 2 + 1) * (NZ // 2)):
                turn = (dy * NZ + place) * NX + dx
                copy = self.message(turn, self.peers.level(place) * PLANE + plane)
                if dy > 0 or place > 0:
                    copy.start()
                else:

                    @pl.when(dx > 0)
                    def _():
                        copy.start()

    def arrived(self, chunk):
        @pl.loop(max(1, 2 * PLANE * chunk), 2 * PLANE * (chunk + 1))
        def _(turn):
            self.message(turn, 0).wait_recv()

    def sent(self):
        @pl.loop(1, NGROUP)
        def _(turn):
            self.message(turn, 0).wait_send()


def iota(shape, dim):
    return lax.broadcasted_iota(I32, shape, dim)


def rows_of(start, count=FOLD):
    return pl.ds(pl.multiple_of(start, FOLD), count)


def to_column(row, count):
    same = iota((count, 128), 0) == iota((count, 128), 1)
    return jnp.sum(jnp.where(same, jnp.broadcast_to(row, (count, 128)), 0), axis=1, keepdims=True)


def matmul(left, right):
    return jnp.dot(left, right, preferred_element_type=F32)


def matmul_t(left, right):
    return lax.dot_general(left, right, (((1,), (1,)), ((), ())), preferred_element_type=F32)


def embed(states, gain, out, inverses):
    @pl.loop(0, PAD // FOLD)
    def _(step):
        at = rows_of(step * FOLD)
        values = states[at, :].astype(F32)
        inverse = lax.rsqrt(jnp.mean(values * values, axis=-1, keepdims=True) + EPSILON)
        inverses[at, :] = inverse
        out[at, :] = (values * inverse * gain[...]).astype(BF)


def place_own(blk, embedded, head, tail):
    head[blk] = embedded[0:HEAD, :]
    last = embedded[HEAD:PAD, :]
    last = last.astype(F32)[0 : ROWS - HEAD]
    tail[blk] = jnp.concatenate([last[:, :TAILW], last[:, TAILW:]], axis=0).astype(BF)


def fold_rows(left, right, factor, swap, work, stage, flat, chunk):
    first = chunk * CROWS

    @pl.loop(0, FOLD)
    def _(k):
        cols = pl.ds(pl.multiple_of(k * FOLDW, FOLDW), FOLDW)
        found = matmul(left, right[:, cols])
        if factor is not None:
            found = factor * found
        found = found.astype(BF)
        if flat is not None:
            flat[rows_of(first, CROWS), cols] = found
        work[:, rows_of(k * FOLD), :] = found.reshape(CROWS // FOLD, FOLD, FOLDW)

    for g in range(CROWS // FOLD):
        folded = matmul(swap[...], work[g]).astype(BF)
        stage[pl.ds(first + g * FOLD, FOLD)] = folded.reshape(FOLD, FOLD, FOLDW)


def pair_scores(embedded, head, tail):
    main = matmul_t(embedded[...], head[...].reshape(HEADS, WIDTH)) * SCALE
    folded = tail[...].reshape(TAILS, TAILW)
    low = matmul_t(embedded[:, :TAILW], folded)
    high = matmul_t(embedded[:, TAILW:], folded)
    return main, (low + pltpu.roll(high, TAILS - (ROWS - HEAD), 1)) * SCALE


def pair_masks(blk):
    row, lane = iota((PAD, HEADS), 0), iota((PAD, HEADS), 1)
    main = (row < HEAD) & (lane == blk * HEAD + row)
    row, lane = iota((PAD, TAILS), 0), iota((PAD, TAILS), 1)
    valid = (lane // (ROWS - HEAD)) % 2 == 0
    rest = (row >= HEAD) & (row < ROWS) & (lane == blk * FOLD + row - HEAD)
    return main, rest, valid


def pair_grads(main, rest, head, tail, out, extra):
    low = rest.astype(BF)
    high = pltpu.roll(rest, ROWS - HEAD, 1).astype(BF)
    main = main.astype(BF)
    for part, coeff in enumerate((low, high)):

        @pl.loop(0, TAILW // STRIP)
        def _(step):
            near = pl.ds(pl.multiple_of(step * STRIP, STRIP), STRIP)
            cols = pl.ds(pl.multiple_of(part * TAILW + step * STRIP, STRIP), STRIP)
            found = matmul(main, head[:, :, cols].reshape(HEADS, STRIP))
            found = found + matmul(coeff, tail[:, :, near].reshape(TAILS, STRIP))
            if extra is not None:
                found = found + extra(cols)
            out[:, cols] = SCALE * found


def norm_backward(states, inverses, gain, upstream, out, gain_sum):
    def rows(at, count):
        values, inverse, given = states[at, :].astype(F32), inverses[at, :], upstream[at, :]
        if out is not None:
            scaled = gain[...] * given
            inner = jnp.sum(scaled * values, axis=-1, keepdims=True)
            found = scaled * inverse - values * inverse**3 * inner / WIDTH
            out[pl.ds(at.start, count), :] = found[:count]
        if gain_sum is not None:
            gain_sum[...] += given * values * inverse

    @pl.loop(0, HEAD // FOLD)
    def _(step):
        rows(rows_of(step * FOLD), FOLD)

    rows(pl.ds(HEAD, FOLD), ROWS - HEAD)


def requests(me, owner, row, ask):
    turns = [turn_of(me, owner[:, k : k + 1]) for k in range(owner.shape[1])]
    down, across = iota((ROWS, 128), 0), iota((ROWS, 128), 1)
    lines = [jnp.sum(jnp.where(down == across, turn, 0), axis=0, keepdims=True) for turn in turns]
    found = jnp.zeros((1, LANES), I32)
    for k, turn in enumerate(turns):
        earlier = jnp.where((turn == lines[k]) & (across < down), 1, 0)
        for line in lines[:k]:
            earlier = earlier + jnp.where((turn == line) & (across < ROWS), 1, 0)
        rank = jnp.sum(earlier, axis=1, keepdims=True)
        lane = (turn // 16) * 128 + (turn % 16) * SLOTS + rank
        hit = lane == iota((ROWS, LANES), 1)
        found = found + jnp.sum(jnp.where(hit, row[:, k : k + 1] + 1, 0), axis=0, keepdims=True)
    ask[...] = found


def kernel(
    both, gain, owner, row_asked,
    query_grad, passage_grad, sums,
    query, passage, ask, query_embed, passage_embed, query_inv, passage_inv, swap,
    phead, ptail, qhead, qtail,
    asked, mine, work, stage, landed, pool, pool_raw, pool_inv, pool_scores, pool_turned,
    terms, term_stage, term_landed,
    main_scores, rest_scores, total_out, totals, query_up, passage_up, gain_sum, held, run,
    ask_send, ask_recv, row_send, row_recv, term_send, term_recv,
    p_send, p_recv, q_send, q_recv, total_send, total_recv, sum_send, sum_recv,
):
    me, blk = lax.axis_index("group"), lax.axis_index("blk")
    z, plane = me // PLANE, me % PLANE
    barrier = pltpu.get_barrier_semaphore()

    there, back = Peers(me), Peers(me, True)

    there.all(
        lambda turn, other: pl.semaphore_signal(
            barrier, inc=1, device_id={"group": other}, device_id_type=MESH
        )
    )

    for d in range(1, NBLK):
        pl.semaphore_signal(barrier, inc=1, device_id={"blk": (blk + d) % NBLK}, device_id_type=MESH)

    requests(me, owner, row_asked, ask)
    asked[0] = ask[...]
    query[0:HEAD] = both[0:HEAD]
    passage[0:HEAD] = both[HEAD : 2 * HEAD]
    last, none = both[2 * HEAD : 2 * ROWS].astype(F32), jnp.zeros((PAD - ROWS, WIDTH), F32)
    query[HEAD:PAD] = jnp.concatenate([last[: ROWS - HEAD], none], axis=0).astype(BF)
    passage[HEAD:PAD] = jnp.concatenate([last[ROWS - HEAD :], none], axis=0).astype(BF)
    embed(passage, gain, passage_embed, passage_inv)
    place_own(blk, passage_embed, phead, ptail)
    row, col = iota((FOLDW, FOLDW), 0), iota((FOLDW, FOLDW), 1)
    same = (row // FOLD == col % FOLD) & (row % FOLD == col // FOLD)
    swap[...] = jnp.where(same, 1.0, 0.0).astype(BF)
    turns = iota((NGROUP, 1, LANES), 0)
    past = iota((NGROUP, 1, LANES), 2) - (turns // 16) * 128 - (turns % 16) * SLOTS
    mine[...] = jnp.where((past >= 0) & (past < SLOTS), 1, 0)
    pl.semaphore_wait(barrier, NGROUP - 1 + NBLK - 1)

    def asking(turn, other):
        return remote(ask, asked.at[turn], ask_send.at[turn], ask_recv.at[turn], group=other)

    there.all(lambda turn, other: asking(turn, other).start())

    ps = Spread(blk, phead, ptail, p_send, p_recv)
    qs = Spread(blk, qhead, qtail, q_send, q_recv)
    ps.hop(0, 1)
    embed(query, gain, query_embed, query_inv)
    place_own(blk, query_embed, qhead, qtail)

    @pl.loop(1, NGROUP)
    def _(turn):
        asking(turn, 0).wait()

    wanted = jnp.sum(asked[...] * mine[...], axis=0)

    rows = Swap(back, stage, landed, row_send, row_recv)
    spread_steps = [
        lambda: ps.hop(4),
        lambda: ps.hop(2),
        lambda: ps.hop(3),
        lambda: (ps.over(2, blk), ps.relay(0)),
        lambda: ps.relay(1),
        lambda: ps.relay(4),
        lambda: ps.pass_near(),
        lambda: None,
    ]
    for step in range(CHUNKS):
        chunk = ORDER[step]
        column = to_column(wanted[:, chunk * 128 : (chunk + 1) * 128], CROWS)
        pick = jnp.where(column - 1 == iota((CROWS, PAD), 1), 1.0, 0.0).astype(BF)
        fold_rows(pick, passage, None, swap, work, stage, None, chunk)
        for half in range(2):
            rows.start(chunk, half)
            spread_steps[2 * step + half]()
    landed[0:SLOTS] = stage[0:SLOTS]
    qs.hop(0, 1, 4)
    main_hit, rest_hit, rest_valid = pair_masks(blk)

    for step in range(CHUNKS):
        chunk = ORDER[step]
        if step == 1:
            ps.pass_far()
        if step == 2:
            ps.finish()
            main, rest = pair_scores(query_embed, phead, ptail)
            main_scores[...] = main
            rest_scores[...] = jnp.where(rest_valid, rest, -jnp.inf)
        rows.arrived(chunk)

        @pl.loop(0, CROWS // FOLD)
        def _(g):
            at = chunk * CROWS + g * FOLD
            tile = landed[pl.ds(at, FOLD)].reshape(FOLDW, FOLDW)
            flat = matmul(swap[...], tile)
            square = jnp.zeros((FOLD, FOLDW), F32)
            for k in range(FOLD):
                part = flat[k * FOLD : (k + 1) * FOLD]
                square = square + part * part
            inverse = lax.rsqrt(jnp.sum(square, axis=1, keepdims=True) / WIDTH + EPSILON)
            pool_inv[rows_of(at), :] = inverse
            for k in range(FOLD):
                part, cols = flat[k * FOLD : (k + 1) * FOLD], slice(k * FOLDW, (k + 1) * FOLDW)
                pool_raw[rows_of(at), cols] = part.astype(BF)
                pool[rows_of(at), cols] = (part * inverse * gain[:, cols]).astype(BF)

        here = pl.ds(chunk * CROWS, CROWS)
        pool_scores[chunk, :, 0:CROWS] = matmul_t(query_embed[...], pool[here, :]) * SCALE
        pool_turned[chunk, :, 0:PAD] = matmul_t(pool[here, :], query_embed[...]) * SCALE

    live = [ask[:, c * 128 : c * 128 + CROWS] > 0 for c in range(CHUNKS)]
    masked = [
        jnp.where(live[c], pool_scores[c, :, 0:CROWS], -jnp.inf) for c in range(CHUNKS)
    ]
    main, rest = main_scores[...], rest_scores[...]
    peak = jnp.maximum(
        jnp.max(main, axis=1, keepdims=True), jnp.max(rest, axis=1, keepdims=True)
    )
    for c in range(CHUNKS):
        peak = jnp.maximum(peak, jnp.max(masked[c], axis=1, keepdims=True))
    added = jnp.sum(jnp.exp(main - peak), axis=1, keepdims=True)
    added = added + jnp.sum(jnp.exp(rest - peak), axis=1, keepdims=True)
    for c in range(CHUNKS):
        added = added + jnp.sum(jnp.exp(masked[c] - peak), axis=1, keepdims=True)
    total = peak + jnp.log(added)
    square = iota((PAD, 128), 0) == iota((PAD, 128), 1)
    total_row = jnp.sum(jnp.where(square, total, 0.0), axis=0, keepdims=True)

    give = Swap(there, term_stage, term_landed, term_send, term_recv)
    q_steps = [
        lambda: qs.relay(0),
        lambda: qs.relay(4),
        lambda: qs.pass_near(),
        lambda: qs.pass_far(),
    ]
    for step in range(CHUNKS):
        chunk = ORDER[step]
        column = to_column(ask[:, chunk * 128 : (chunk + 1) * 128], CROWS)
        turned = jnp.exp(pool_turned[chunk, :, 0:PAD] - total_row[:, 0:PAD])
        turned = jnp.where(column > 0, turned, 0.0).astype(BF)
        fold_rows(turned, query_embed, SCALE, swap, work, term_stage, terms, chunk)
        give.start(chunk, 0)
        if step == 0:
            qs.hop(2, 3)
            qs.over(2, blk)
        if step == 1:
            qs.relay(1)
        give.start(chunk, 1)
        if step == 0:
            total_out[...] = jnp.concatenate(
                [
                    jnp.sum(jnp.where(main_hit, total, 0.0), axis=0, keepdims=True),
                    jnp.sum(jnp.where(rest_hit, total, 0.0), axis=0, keepdims=True),
                ],
                axis=1,
            )
            totals[blk] = total_out[...]
            total_copies = [
                remote(
                    total_out, totals.at[blk], total_send.at[d], total_recv.at[d],
                    blk=(blk + d) % NBLK,
                )
                for d in range(1, NBLK)
            ]
            for copy in total_copies:
                copy.start()
        q_steps[step]()
    term_landed[0:SLOTS] = term_stage[0:SLOTS]

    gain_sum[...] = jnp.zeros_like(gain_sum)
    main = jnp.exp(main - total) - jnp.where(main_hit, 1.0, 0.0)
    rest = jnp.where(rest_valid, jnp.exp(rest - total), 0.0) - jnp.where(rest_hit, 1.0, 0.0)
    coeffs = [jnp.exp(masked[c] - total).astype(BF) for c in range(CHUNKS)]

    def from_pool(cols):
        found = matmul(coeffs[0], pool[0:CROWS, cols])
        for c in range(1, CHUNKS):
            found = found + matmul(coeffs[c], pool[c * CROWS : (c + 1) * CROWS, cols])
        return found

    pair_grads(main, rest, phead, ptail, query_up, from_pool)
    norm_backward(query, query_inv, gain, query_up, query_grad, gain_sum)

    @pl.loop(0, POOL // FOLD)
    def _(g):
        at = rows_of(g * FOLD)
        gain_sum[...] += terms[at, :].astype(F32) * (pool_raw[at, :].astype(F32) * pool_inv[at, :])

    positive = jnp.sum(jnp.where(main_hit, main_scores[...], 0.0), axis=1, keepdims=True)
    positive = positive + jnp.sum(jnp.where(rest_hit, rest_scores[...], 0.0), axis=1, keepdims=True)
    loss = jnp.where(iota((PAD, 128), 0) < ROWS, total - positive, 0.0)
    loss = jnp.sum(loss, axis=0, keepdims=True)

    def unfold(step):
        chunk = ORDER[step]
        give.arrived(chunk)

        @pl.loop(0, CROWS // FOLD)
        def _(g):
            at = chunk * CROWS + g * FOLD
            tile = term_landed[pl.ds(at, FOLD)].reshape(FOLDW, FOLDW)
            flat = matmul(swap[...], tile).astype(BF)
            for k in range(FOLD):
                terms[rows_of(at), k * FOLDW : (k + 1) * FOLDW] = flat[k * FOLD : (k + 1) * FOLD]

    unfold(0)
    unfold(1)
    qs.finish()
    for copy in total_copies:
        copy.wait()
    lane_totals = totals[0]
    for b in range(1, NBLK):
        lane_totals = lane_totals + totals[b]
    main, rest = pair_scores(passage_embed, qhead, qtail)
    main = jnp.exp(main - lane_totals[:, :HEADS]) - jnp.where(main_hit, 1.0, 0.0)
    rest = jnp.exp(rest - lane_totals[:, HEADS:]) - jnp.where(rest_hit, 1.0, 0.0)
    rest = jnp.where(rest_valid, rest, 0.0)
    pair_grads(main, rest, qhead, qtail, passage_up, None)
    norm_backward(passage, passage_inv, gain, passage_up, None, gain_sum)

    run[0, :, 0:WIDTH] = jnp.sum(gain_sum[...], axis=0, keepdims=True)
    run[0, :, WIDTH:GAINS] = loss
    where = [
        lambda d: {"blk": (blk + d) % NBLK},
        lambda d: {"group": ((z + d) % NZ) * PLANE + plane},
        lambda d: {"group": z * PLANE + (plane + d) % PLANE},
    ]
    slots = (blk, z, plane)

    def sum_copies(level):
        return [
            remote(
                run.at[level], held.at[level, slots[level]],
                sum_send.at[level, d], sum_recv.at[level, d], **where[level](d),
            )
            for d in range(1, 8)
        ]

    def sum_start(level):
        held[level, slots[level]] = run[level]
        for copy in sum_copies(level):
            copy.start()

    def sum_end(level):
        for copy in sum_copies(level):
            copy.wait()
        got = held[level, 0]
        for d in range(1, 8):
            got = got + held[level, d]
        if level < 2:
            run[level + 1] = got
        else:
            sums[...] = got

    sum_start(0)
    unfold(2)
    sum_end(0)
    sum_start(1)
    unfold(3)
    sum_end(1)
    sum_start(2)

    names = [
        jnp.where(iota((PAD, CROWS), 0) + 1 == wanted[:, c * 128 : c * 128 + CROWS], 1.0, 0.0).astype(BF)
        for c in range(CHUNKS)
    ]

    @pl.loop(0, WIDTH // STRIP)
    def _(step):
        cols = pl.ds(pl.multiple_of(step * STRIP, STRIP), STRIP)
        found = passage_up[:, cols]
        for c in range(CHUNKS):
            found = found + matmul(names[c], terms[c * CROWS : (c + 1) * CROWS, cols])
        passage_up[:, cols] = found

    norm_backward(passage, passage_inv, gain, passage_up, passage_grad, None)
    sum_end(2)
    ps.sent()
    qs.sent()
    rows.sent()
    give.sent()


def local(query_states, passage_states, norm_gain, negative_owner, negative_row):
    both = jnp.concatenate(
        [
            query_states[:HEAD], passage_states[:HEAD],
            query_states[HEAD:], passage_states[HEAD:],
        ]
    )
    vmem = pl.BlockSpec(memory_space=pltpu.VMEM)
    dma = pltpu.SemaphoreType.DMA
    query_grad, passage_grad, sums = pl.pallas_call(
        kernel,
        out_shape=(
            jax.ShapeDtypeStruct((ROWS, WIDTH), F32),
            jax.ShapeDtypeStruct((ROWS, WIDTH), F32),
            jax.ShapeDtypeStruct((1, GAINS), F32),
        ),
        in_specs=[vmem] * 4,
        out_specs=(vmem,) * 3,
        scratch_shapes=[
            pltpu.VMEM((PAD, WIDTH), BF),
            pltpu.VMEM((PAD, WIDTH), BF),
            pltpu.VMEM((1, LANES), I32),
            pltpu.VMEM((PAD, WIDTH), BF),
            pltpu.VMEM((PAD, WIDTH), BF),
            pltpu.VMEM((PAD, 1), F32),
            pltpu.VMEM((PAD, 1), F32),
            pltpu.VMEM((FOLDW, FOLDW), BF),
            pltpu.VMEM((NBLK, HEAD, WIDTH), BF),
            pltpu.VMEM((NBLK, FOLD, TAILW), BF),
            pltpu.VMEM((NBLK, HEAD, WIDTH), BF),
            pltpu.VMEM((NBLK, FOLD, TAILW), BF),
            pltpu.VMEM((NGROUP, 1, LANES), I32),
            pltpu.VMEM((NGROUP, 1, LANES), I32),
            pltpu.VMEM((CROWS // FOLD, FOLDW, FOLDW), BF),
            pltpu.VMEM((POOL, FOLD, FOLDW), BF),
            pltpu.VMEM((POOL, FOLD, FOLDW), BF),
            pltpu.VMEM((POOL, WIDTH), BF),
            pltpu.VMEM((POOL, WIDTH), BF),
            pltpu.VMEM((POOL, 1), F32),
            pltpu.VMEM((CHUNKS, PAD, 128), F32),
            pltpu.VMEM((CHUNKS, CROWS, 128), F32),
            pltpu.VMEM((POOL, WIDTH), BF),
            pltpu.VMEM((POOL, FOLD, FOLDW), BF),
            pltpu.VMEM((POOL, FOLD, FOLDW), BF),
            pltpu.VMEM((PAD, HEADS), F32),
            pltpu.VMEM((PAD, TAILS), F32),
            pltpu.VMEM((1, HEADS + TAILS), F32),
            pltpu.VMEM((NBLK, 1, HEADS + TAILS), F32),
            pltpu.VMEM((PAD, WIDTH), F32),
            pltpu.VMEM((PAD, WIDTH), F32),
            pltpu.VMEM((FOLD, WIDTH), F32),
            pltpu.VMEM((3, 8, 1, GAINS), F32),
            pltpu.VMEM((3, 1, GAINS), F32),
            *[dma((NGROUP,))] * 6,
            *[dma((8, 5))] * 4,
            *[dma((NBLK,))] * 2,
            *[dma((3, 8))] * 2,
        ],
        compiler_params=pltpu.CompilerParams(
            collective_id=0, has_side_effects=True, vmem_limit_bytes=VMEM_LIMIT
        ),
    )(both, norm_gain[None, :], negative_owner, negative_row)
    loss = sums[0, WIDTH] / (ROWS * NBLK * NGROUP)
    return (query_grad, passage_grad, sums[0, :WIDTH], loss)

def solution(mesh):
    return jax.shard_map(
        local,
        mesh=mesh,
        in_specs=(
            P(("blk", "group"), None),
            P(("blk", "group"), None),
            P(),
            P(("blk", "group"), None),
            P(("blk", "group"), None),
        ),
        out_specs=(P(("blk", "group"), None), P(("blk", "group"), None), P(), P()),
        check_vma=False,
    )
```
